256 devices in a mesh: rep: 8 (over z), shard: 32 (over x, y, core).
Axes of the slice: x: 4, y: 4, z: 8, core: 2. Of those that a mesh axis runs over, the one named last changes fastest.
Arguments:
- grads: bfloat16 [8, 8192, 8192], P('rep', 'shard'), may hold values from -40 to 40
- owner_table: int32 [32, 32, 1], P('shard'), may hold values from 0 to 31; in each aligned block of 32 rows (0 to 31, 32 to 63, ..., all dimensions but the last counted through in order) at most 2 rows name the same one
- left_roots: float32 [32, 32, 2, 256, 256], P('shard', 'rep'), may hold values from -1 to 2.5
- right_roots: float32 [32, 32, 2, 256, 256], P('shard', 'rep'), may hold values from -1 to 2.5
Outputs:
- direction: bfloat16 [8192, 8192], P('shard')
The draws below stay inside these ranges and needn't reach their ends.
Inputs may be any that keep to these rules, and one draw needn't show every extreme that they name: `owner_table`: among the blocks of the rows of one index of shard (32 blocks), no owner is named more than 2 times, a bound that some block reaches.
All inputs are finite; a program needn't handle non-finite values.
Results may differ from the reference program's by a relative error of at most 0.019.
Values may be sent and summed in bfloat16 or wider, within the bound.
No kernel may reach another device: no remote copies, remote signals or barrier semaphores. Data moves between devices by JAX's collectives and lax.ppermute only.
A program may use at most 128 MiB of HBM per device.

```python
import math
import jax
import jax.numpy as jnp
import numpy as np
from jax import lax

D = 8192
BS = 256
BR_DEV = 1
NBC = 32
NBR = 32
ROWS = 8192
BLK_DEV = 32
CAP = 2
N_REP = 8
N_SHARD = 32


def assemble_root(raw, diag_values):
    symmetric = (raw + jnp.swapaxes(raw, -1, -2)) * (0.32 / (2.0 * BS) ** 0.5)
    identity = jnp.eye(BS, dtype=jnp.float32)
    return symmetric + diag_values[..., None] * identity


def draw_left_roots(key, part):
    key = jax.random.fold_in(key, 11)
    key_raw, key_diag = jax.random.split(key)
    shape = (N_SHARD, N_SHARD, CAP, BS, BS)
    raw = jnp.clip(jax.random.normal(key_raw, shape, jnp.float32), -4.0, 4.0)
    diag_values = jax.random.uniform(key_diag, shape[:-1], jnp.float32, 1.0, 2.0)
    return assemble_root(raw, diag_values)


def draw_right_roots(key, part):
    key = jax.random.fold_in(key, 23)
    key_raw, key_diag = jax.random.split(key)
    shape = (N_SHARD, N_SHARD, CAP, BS, BS)
    raw = jnp.clip(jax.random.normal(key_raw, shape, jnp.float32), -4.0, 4.0)
    diag_values = jax.random.uniform(key_diag, shape[:-1], jnp.float32, 1.0, 2.0)
    return assemble_root(raw, diag_values)


def draw_grads(key, part):
    key = jax.random.fold_in(key, 5)
    key_row, key_col, key_noise = jax.random.split(key, 3)
    row_scale = jnp.exp(jax.random.uniform(key_row, (ROWS,), jnp.float32, -1.2, 1.1))
    col_scale = jnp.exp(jax.random.uniform(key_col, (D,), jnp.float32, -1.2, 1.1))
    shape = (N_REP, ROWS, D)
    values = jnp.clip(jax.random.normal(key_noise, shape, jnp.float32), -4.0, 4.0)
    return (values * row_scale[None, :, None] * col_scale[None, None, :]).astype(jnp.bfloat16)


def deal_out(own_key, own, number, rows, count, top, bound, slope):
    sequence = jax.random.permutation(own_key, count)
    crowded, ordinary = portions_of(count, rows * top, bound, slope, True), portions_of(count, rows * top, bound, slope, False)
    places = jnp.arange(count)

    def named(tallies, offset_by):
        used = int((tallies > 0).sum())
        fixed = max(1, used // 4)
        shifted = fixed + (places - fixed + offset_by * (used - fixed)) % max(1, count - fixed)
        return jnp.zeros((count,), jnp.int32).at[sequence[jnp.where(places < fixed, places, shifted)]].set(jnp.asarray(tallies, jnp.int32))

    tallies = jnp.where(number % 4 == 0, named(crowded, number // 4), named(ordinary, number - number // 4 - 1))
    mixed = jax.random.permutation(jax.random.fold_in(own, 3), count)
    giver, taker = mixed[0:count // 2 * 2:2], mixed[1:count // 2 * 2:2]
    slack = jnp.minimum(tallies[giver] - 1, bound - tallies[taker]) // 2
    slack = jnp.where((giver == sequence[0]) | (taker == sequence[0]) | (tallies[taker] == 0), 0, jnp.maximum(slack, 0))
    shifted = jax.random.randint(jax.random.fold_in(own, 4), (count // 2,), 0, 1 << 20) % (slack + 1)
    tallies = tallies.at[giver].add(-shifted).at[taker].add(shifted)
    items = jnp.searchsorted(jnp.cumsum(tallies), jnp.arange(rows * top), side="right").astype(jnp.int32)
    table = items.reshape(top, rows).T
    table = table[jax.random.permutation(jax.random.fold_in(own, 1), rows)]
    offset_by = jax.random.randint(jax.random.fold_in(own, 2), (rows, 1), 0, top)
    return jnp.take_along_axis(table, (jnp.arange(top)[None, :] + offset_by) % top, axis=1)


def portions_of(amount, total, limit, skew, full):
    portions = [(1 << 20) // math.isqrt(rank ** skew) + 1 for rank in range(1, amount + 1)]
    largest = limit if full else min(limit, max(-(-total // amount), total * portions[0] // sum(portions)))
    least = 1 if total - largest >= amount - 1 else 0
    given, surplus = [largest] + [least] * (amount - 1), total - largest - least * (amount - 1)
    while surplus > 0:
        free = [i for i in range(1, amount) if given[i] < largest] or [i for i in range(1, amount) if given[i] < limit]
        mass, remaining = sum([portions[i] for i in free]), surplus
        for i in free:
            addition = min(limit - given[i], max(1, remaining * portions[i] // mass), surplus)
            given[i] = given[i] + addition
            surplus = surplus - addition
    return np.array(given)


def setup_inputs(seed: int = 0) -> dict:
    streams_of = jax.random.split(jax.random.key(seed), 5)
    grads = draw_grads(jax.random.fold_in(streams_of[4], 71), 0)
    owner_table_keys = jax.random.split(jax.random.fold_in(streams_of[1], 1), NBR * NBC // BLK_DEV)
    owner_table_turns = jax.random.permutation(jax.random.fold_in(streams_of[1], 3), NBR * NBC // BLK_DEV)
    owner_table = jax.vmap(lambda own, number: deal_out(jax.random.fold_in(streams_of[1], 2), own, number, BLK_DEV, N_SHARD, 1, CAP, 2))(owner_table_keys, owner_table_turns).reshape((NBR, NBC, 1))
    left_roots = draw_left_roots(jax.random.fold_in(streams_of[4], 71), 0)
    right_roots = draw_right_roots(jax.random.fold_in(streams_of[4], 71), 0)
    return dict(grads=grads, owner_table=owner_table, left_roots=left_roots, right_roots=right_roots)


EPS = 1e-06

def precondition(tile, left_root, right_root):
    grad_tile = lax.optimization_barrier(tile).astype(jnp.float32)
    partial_prod = jnp.dot(grad_tile, right_root, precision=lax.Precision.HIGHEST)
    precond = jnp.dot(left_root, partial_prod, precision=lax.Precision.HIGHEST)
    scale = jnp.sqrt(jnp.mean(grad_tile * grad_tile) + EPS) / jnp.sqrt(jnp.mean(precond * precond) + EPS)
    return (precond * scale).astype(jnp.bfloat16)

def reference(grads, owner_table, left_roots, right_roots):
    mean_grad = (lax.optimization_barrier(jnp.sum(grads, axis=0, dtype=jnp.float32)) / N_REP).astype(jnp.bfloat16)
    block_rows = mean_grad.shape[0] // BS
    block_cols = mean_grad.shape[1] // BS
    total_blocks = block_rows * block_cols
    per_device = BR_DEV * block_cols
    tiles = mean_grad.reshape(block_rows, BS, block_cols, BS).transpose(0, 2, 1, 3).reshape(total_blocks, BS, BS)
    owners = owner_table.reshape(N_SHARD, per_device).astype(jnp.int32)
    one_hot = (owners[:, :, None] == jnp.arange(N_SHARD, dtype=jnp.int32)[None, None, :]).astype(jnp.int32)
    ranking = jnp.cumsum(one_hot, axis=1).astype(jnp.int32) - one_hot
    slot_index = lax.optimization_barrier(jnp.sum(ranking * one_hot, axis=2)).astype(jnp.int32).reshape(-1)
    senders = (jnp.arange(total_blocks, dtype=jnp.int32) // per_device).astype(jnp.int32)
    owner_flat = owners.reshape(-1)

    def handle(entry):
        tile, owner, sender, slot = entry
        return precondition(tile, left_roots[owner, sender, slot], right_roots[owner, sender, slot])
    result = lax.map(handle, (tiles, owner_flat, senders, slot_index))
    return result.reshape(block_rows, block_cols, BS, BS).transpose(0, 2, 1, 3).reshape(block_rows * BS, block_cols * BS)
```

```python
import functools

import jax
import jax.numpy as jnp
from jax import lax
from jax.experimental import pallas as pl
from jax.experimental.pallas import tpu as pltpu
from jax.sharding import Mesh, PartitionSpec as P

BS = 256
EPS = 1e-06
GROUP = 4
VMEM_LIMIT = 32 * 1024 * 1024


def copy_all(copies):
    for copy in copies:
        copy.start()
    for copy in copies:
        copy.wait()


def place_kernel(index, wide, blocks, sems):
    copy_all(
        [
            pltpu.make_async_copy(
                wide.at[:, pl.ds(c * BS, BS)], blocks.at[index[c]], sems.at[c]
            )
            for c in range(blocks.shape[0])
        ]
    )


def spread_kernel(index, blocks, wide, sems):
    copy_all(
        [
            pltpu.make_async_copy(
                blocks.at[index[c]], wide.at[:, pl.ds(c * BS, BS)], sems.at[c]
            )
            for c in range(blocks.shape[0])
        ]
    )


def pick_kernel(index, source, target, sems):
    copy_all(
        [
            pltpu.make_async_copy(source.at[index[n]], target.at[n], sems.at[n])
            for n in range(target.shape[0])
        ]
    )


def moved(kernel, index, operand, shape, name):
    return pl.pallas_call(
        kernel,
        out_shape=jax.ShapeDtypeStruct(shape, operand.dtype),
        in_specs=[
            pl.BlockSpec(memory_space=pltpu.SMEM),
            pl.BlockSpec(memory_space=pl.ANY),
        ],
        out_specs=pl.BlockSpec(memory_space=pl.ANY),
        scratch_shapes=[pltpu.SemaphoreType.DMA((index.shape[0],))],
        compiler_params=pltpu.CompilerParams(vmem_limit_bytes=VMEM_LIMIT),
        name=name,
    )(index, operand)


def pick(index, operand, name):
    return moved(pick_kernel, index, operand, index.shape + operand.shape[1:], name)


def split(value):
    high = value.astype(jnp.bfloat16)
    return high, (value - high.astype(jnp.float32)).astype(jnp.bfloat16)


def precondition_kernel(inverse_count, total, roots, result):
    dot = functools.partial(jnp.dot, preferred_element_type=jnp.float32)
    grad = (total[0].astype(jnp.float32) * inverse_count).astype(jnp.bfloat16)
    left, right = roots[0, 0], roots[0, 1]
    high, low = split(dot(grad, right))
    precond = dot(left, high) + dot(left, low)
    wide = grad.astype(jnp.float32)
    scale = jnp.sqrt(jnp.mean(wide * wide) + EPS) / jnp.sqrt(
        jnp.mean(precond * precond) + EPS
    )
    result[0] = (precond * scale).astype(jnp.bfloat16)


def precondition(total, roots, count):
    blocks = total.shape[0]
    return pl.pallas_call(
        functools.partial(precondition_kernel, 1.0 / count),
        grid=(blocks,),
        out_shape=jax.ShapeDtypeStruct(total.shape, jnp.bfloat16),
        in_specs=[
            pl.BlockSpec((1, BS, BS), lambda n: (n, 0, 0)),
            pl.BlockSpec((1, 2, BS, BS), lambda n: (n, 0, 0, 0)),
        ],
        out_specs=pl.BlockSpec((1, BS, BS), lambda n: (n, 0, 0)),
        compiler_params=pltpu.CompilerParams(vmem_limit_bytes=VMEM_LIMIT),
        name="precondition",
    )(total, roots)


def local(grads, owner_table, left_roots, right_roots):
    replicas = lax.axis_size("rep")
    groups = lax.axis_size("g")
    members = lax.axis_size("j")
    width = grads.shape[2]
    count = width // BS
    capacity = left_roots.shape[2]
    per_replica = count // replicas
    owners = owner_table.reshape(count)
    my_rep = lax.axis_index("rep")
    my_group = lax.axis_index("g")

    order = jnp.arange(count, dtype=jnp.int32)
    before = (owners[None, :] < owners[:, None]) | (
        (owners[None, :] == owners[:, None]) & (order[None, :] < order[:, None])
    )
    place = jnp.sum(before.astype(jnp.int32), axis=1)
    stored = (place % replicas) * per_replica + place // replicas
    ordered = moved(place_kernel, stored, grads[0], (count, BS, BS), "place")
    total = lax.psum_scatter(ordered, "rep", scatter_dimension=0, tiled=True)

    roots = jnp.stack([left_roots[0], right_roots[0]], axis=2).astype(jnp.bfloat16)
    roots = lax.all_to_all(roots, "j", split_axis=0, concat_axis=0, tiled=True)
    tables = lax.all_gather(owners, "g", axis=0)
    sender = lax.dynamic_index_in_dim(tables, my_rep, axis=0, keepdims=False)
    slot_owner = my_group * members + jnp.arange(members, dtype=jnp.int32)
    first = jnp.sum((sender[None, :] < slot_owner[:, None]).astype(jnp.int32), axis=1)
    named = jnp.sum((sender[None, :] == slot_owner[:, None]).astype(jnp.int32), axis=1)
    slot = jnp.arange(capacity, dtype=jnp.int32)
    slot_place = (first[:, None] + slot[None, :]).reshape(-1)
    slot_used = (slot[None, :] < named[:, None]).reshape(-1)
    slot_order = jnp.arange(members * capacity, dtype=jnp.int32)
    taken = slot_used[None, :] & (
        slot_place[None, :] % replicas == jnp.arange(replicas, dtype=jnp.int32)[:, None]
    )
    root_index = jnp.sum(jnp.where(taken, slot_order[None, :], 0), axis=1)
    roots = pick(
        root_index, roots.reshape(members * capacity, 2, BS, BS), "pick_roots"
    )
    roots = lax.all_to_all(roots, "rep", split_axis=0, concat_axis=0, tiled=True)

    held = my_rep + replicas * jnp.arange(per_replica, dtype=jnp.int32)
    held_group = jnp.sum(
        jnp.where(place[None, :] == held[:, None], owners[None, :], 0), axis=1
    ) // members
    here = held_group[None, :] == jnp.arange(groups, dtype=jnp.int32)[:, None]
    block_index = jnp.sum(
        jnp.where(here, jnp.arange(per_replica, dtype=jnp.int32)[None, :], 0), axis=1
    )
    sent = lax.all_to_all(
        pick(block_index, total, "pick_blocks"), "g", split_axis=0, concat_axis=0, tiled=True
    )
    outcome = precondition(sent, roots, replicas)
    back = lax.all_to_all(outcome, "g", split_axis=0, concat_axis=0, tiled=True)
    mine = pick(held_group, back, "pick_results")
    gathered = lax.all_gather(mine, "rep", axis=0, tiled=True)
    return moved(spread_kernel, stored, gathered, (BS, width), "spread")


def solution(mesh):
    replicas, shards = mesh.shape["rep"], mesh.shape["shard"]
    fine = Mesh(
        mesh.devices.reshape(replicas, shards // GROUP, GROUP), ("rep", "g", "j")
    )
    shard = ("g", "j")
    placed = (
        P("rep", shard, None),
        P(shard, None, None),
        P(shard, "rep", None, None, None),
        P(shard, "rep", None, None, None),
    )
    return jax.shard_map(
        local, mesh=fine, in_specs=placed, out_specs=P(shard, None), check_vma=False
    )
```

```python
import functools

import jax
import jax.numpy as jnp
from jax import lax
from jax.experimental import pallas as pl
from jax.experimental.pallas import tpu as pltpu
from jax.sharding import Mesh, PartitionSpec as P

BS = 256
EPS = 1e-06
GROUP = 4
VMEM_LIMIT = 32 * 1024 * 1024


def copy_all(copies):
    for copy in copies:
        copy.start()
    for copy in copies:
        copy.wait()


def place_kernel(index, wide, blocks, sems):
    copy_all(
        [
            pltpu.make_async_copy(
                wide.at[:, pl.ds(c * BS, BS)], blocks.at[index[c]], sems.at[c]
            )
            for c in range(blocks.shape[0])
        ]
    )


def spread_kernel(index, blocks, wide, sems):
    copy_all(
        [
            pltpu.make_async_copy(
                blocks.at[index[c]], wide.at[:, pl.ds(c * BS, BS)], sems.at[c]
            )
            for c in range(blocks.shape[0])
        ]
    )


def pick_kernel(index, source, *rest):
    target, sems = rest[-2:]
    copy_all(
        [
            pltpu.make_async_copy(source.at[index[n]], target.at[n], sems.at[n])
            for n in range(target.shape[0])
        ]
    )


def fan_kernel(index, source, *rest):
    targets, sems = rest[:-1], rest[-1]
    copy_all(
        [
            pltpu.make_async_copy(source.at[index[n]], target, sems.at[n])
            for n, target in enumerate(targets)
        ]
    )


def moved(kernel, index, operand, shapes, name, after=()):
    out = jax.tree.map(
        lambda shape: jax.ShapeDtypeStruct(shape, operand.dtype),
        shapes,
        is_leaf=lambda leaf: isinstance(leaf, tuple),
    )
    return pl.pallas_call(
        kernel,
        out_shape=out,
        in_specs=[pl.BlockSpec(memory_space=pltpu.SMEM)]
        + [pl.BlockSpec(memory_space=pl.ANY)] * (1 + len(after)),
        out_specs=jax.tree.map(lambda _: pl.BlockSpec(memory_space=pl.ANY), out),
        scratch_shapes=[pltpu.SemaphoreType.DMA((index.shape[0],))],
        compiler_params=pltpu.CompilerParams(vmem_limit_bytes=VMEM_LIMIT),
        name=name,
    )(index, operand, *after)


def pick(index, operand, name, after=()):
    return moved(pick_kernel, index, operand, index.shape + operand.shape[1:], name, after)


def fan(index, operand, name):
    return moved(fan_kernel, index, operand, [operand.shape[1:]] * index.shape[0], name)


def pack_kernel(left, right, both):
    def step(n, carry):
        both[n, 0] = left[n].astype(jnp.bfloat16)
        both[n, 1] = right[n].astype(jnp.bfloat16)
        return carry

    lax.fori_loop(0, left.shape[0], step, 0)


def pack(left, right):
    blocks = left.shape[0]
    vmem = pl.BlockSpec(memory_space=pltpu.VMEM)
    return pl.pallas_call(
        pack_kernel,
        out_shape=jax.ShapeDtypeStruct((blocks, 2, BS, BS), jnp.bfloat16),
        in_specs=[vmem, vmem],
        out_specs=vmem,
        compiler_params=pltpu.CompilerParams(vmem_limit_bytes=VMEM_LIMIT),
        name="pack",
    )(left, right)


def split(value):
    high = value.astype(jnp.bfloat16)
    return high, (value - high.astype(jnp.float32)).astype(jnp.bfloat16)


def precondition_kernel(inverse_count, index, roots, *rest):
    totals, result = rest[:-1], rest[-1]
    dot = functools.partial(jnp.dot, preferred_element_type=jnp.float32)
    for n, total in enumerate(totals):
        at = index[n]
        grad = (total[...].astype(jnp.float32) * inverse_count).astype(jnp.bfloat16)
        left, right = roots[at, 0], roots[at, 1]
        high, low = split(dot(grad, right))
        precond = dot(left, high) + dot(left, low)
        wide = grad.astype(jnp.float32)
        scale = jnp.sqrt(jnp.mean(wide * wide) + EPS) / jnp.sqrt(
            jnp.mean(precond * precond) + EPS
        )
        result[at] = (precond * scale).astype(jnp.bfloat16)


def precondition(index, roots, totals, count):
    blocks = len(totals)
    vmem = pl.BlockSpec(memory_space=pltpu.VMEM)
    return pl.pallas_call(
        functools.partial(precondition_kernel, 1.0 / count),
        out_shape=jax.ShapeDtypeStruct((blocks, BS, BS), jnp.bfloat16),
        in_specs=[pl.BlockSpec(memory_space=pltpu.SMEM)] + [vmem] * (1 + blocks),
        out_specs=vmem,
        compiler_params=pltpu.CompilerParams(vmem_limit_bytes=VMEM_LIMIT),
        cost_estimate=pl.CostEstimate(
            flops=6 * blocks * BS**3, bytes_accessed=8 * blocks * BS**2, transcendentals=0
        ),
        name="precondition",
    )(index, roots, *totals)


def local(grads, owner_table, left_roots, right_roots):
    replicas = lax.axis_size("rep")
    groups = lax.axis_size("g")
    members = lax.axis_size("j")
    width = grads.shape[2]
    count = width // BS
    capacity = left_roots.shape[2]
    per_replica = count // replicas
    owners = owner_table.reshape(count)
    my_rep = lax.axis_index("rep")
    my_group = lax.axis_index("g")

    sender = lax.ppermute(
        owner_table.reshape(1, count),
        ("rep", "g"),
        [(a * groups + b, b * groups + a) for a in range(replicas) for b in range(groups)],
    ).reshape(count)

    order = jnp.arange(count, dtype=jnp.int32)
    before = (owners[None, :] < owners[:, None]) | (
        (owners[None, :] == owners[:, None]) & (order[None, :] < order[:, None])
    )
    place = jnp.sum(before.astype(jnp.int32), axis=1)
    stored = (place % replicas) * per_replica + place // replicas
    ordered = moved(place_kernel, stored, grads[0], (count, BS, BS), "place")
    total = lax.psum_scatter(ordered, "rep", scatter_dimension=0, tiled=True)

    roots = pack(
        left_roots.reshape(members * capacity, BS, BS),
        right_roots.reshape(members * capacity, BS, BS),
    ).reshape(members, capacity, 2, BS, BS)
    roots = lax.all_to_all(roots, "j", split_axis=0, concat_axis=0, tiled=True)
    slot_owner = my_group * members + jnp.arange(members, dtype=jnp.int32)
    first = jnp.sum((sender[None, :] < slot_owner[:, None]).astype(jnp.int32), axis=1)
    named = jnp.sum((sender[None, :] == slot_owner[:, None]).astype(jnp.int32), axis=1)
    slot = jnp.arange(capacity, dtype=jnp.int32)
    slot_place = (first[:, None] + slot[None, :]).reshape(-1)
    slot_used = (slot[None, :] < named[:, None]).reshape(-1)
    slot_order = jnp.arange(members * capacity, dtype=jnp.int32)
    taken = slot_used[None, :] & (
        slot_place[None, :] % replicas == jnp.arange(replicas, dtype=jnp.int32)[:, None]
    )
    root_index = jnp.sum(jnp.where(taken, slot_order[None, :], 0), axis=1)
    roots = pick(
        root_index, roots.reshape(members * capacity, 2, BS, BS), "pick_roots"
    )
    roots = lax.all_to_all(roots, "rep", split_axis=0, concat_axis=0, tiled=True)

    held = my_rep + replicas * jnp.arange(per_replica, dtype=jnp.int32)
    held_group = jnp.sum(
        jnp.where(place[None, :] == held[:, None], owners[None, :], 0), axis=1
    ) // members
    partner = my_group ^ jnp.arange(groups, dtype=jnp.int32)
    here = held_group[None, :] == partner[:, None]
    block_index = jnp.sum(
        jnp.where(here, jnp.arange(per_replica, dtype=jnp.int32)[None, :], 0), axis=1
    )
    sent = fan(block_index, total, "fan_blocks")
    totals = [sent[0]] + [
        lax.ppermute(sent[n], "g", [(a, a ^ n) for a in range(groups)])
        for n in range(1, groups)
    ]
    outcome = precondition(partner, roots, totals, replicas)
    back = lax.all_to_all(outcome, "g", split_axis=0, concat_axis=0, tiled=True)
    mine = pick(held_group, back, "pick_results")
    gathered = lax.all_gather(mine, "rep", axis=0, tiled=True)
    return moved(spread_kernel, stored, gathered, (BS, width), "spread")


def solution(mesh):
    replicas, shards = mesh.shape["rep"], mesh.shape["shard"]
    fine = Mesh(
        mesh.devices.reshape(replicas, shards // GROUP, GROUP), ("rep", "g", "j")
    )
    shard = ("g", "j")
    placed = (
        P("rep", shard, None),
        P(shard, None, None),
        P(shard, "rep", None, None, None),
        P(shard, "rep", None, None, None),
    )
    return jax.shard_map(
        local, mesh=fine, in_specs=placed, out_specs=P(shard, None), check_vma=False
    )
```

```python
import functools

import jax
import jax.numpy as jnp
import numpy as np
from jax import lax
from jax.experimental import pallas as pl
from jax.experimental.pallas import tpu as pltpu
from jax.sharding import Mesh, PartitionSpec as P

BS = 256
EPS = 1e-06
GROUP = 4
REPLICAS = 8
VMEM_LIMIT = 32 * 1024 * 1024

STEPS = np.array(
    [
        [(0, 0), (2, 2), (1, 3), (3, 1), (4, 4), (-2, -2), (-1, -3), (-3, -1)],
        [(4, 4), (-2, -2), (-1, -3), (-3, -1), (0, 0), (2, 2), (1, 3), (3, 1)],
    ],
    dtype=np.int32,
)
REPLICA_AT = np.array(
    [
        [[(m + steps[m % 2]) % REPLICAS for m in range(REPLICAS)] for steps in columns]
        for columns in STEPS
    ],
    dtype=np.int32,
)


def along_rep():
    return [
        ((m * REPLICAS + g) * GROUP + j, (int(REPLICA_AT[j % 2, g, m]) * REPLICAS + g) * GROUP + j)
        for m in range(REPLICAS)
        for g in range(REPLICAS)
        for j in range(GROUP)
    ]


def in_plane():
    return [
        ((int(REPLICA_AT[j % 2, g, m]) * REPLICAS + m) * GROUP + j,
         (int(REPLICA_AT[j % 2, g, m]) * REPLICAS + g) * GROUP + j)
        for m in range(REPLICAS)
        for g in range(REPLICAS)
        for j in range(GROUP)
    ]


def copy_all(copies):
    for copy in copies:
        copy.start()
    for copy in copies:
        copy.wait()


def place_kernel(index, wide, *rest):
    blocks, sems = rest[-2:]
    copy_all(
        [
            pltpu.make_async_copy(
                wide.at[:, pl.ds(c * BS, BS)], blocks.at[index[c]], sems.at[c]
            )
            for c in range(blocks.shape[0])
        ]
    )


def spread_kernel(index, blocks, wide, sems):
    copy_all(
        [
            pltpu.make_async_copy(
                blocks.at[index[c]], wide.at[:, pl.ds(c * BS, BS)], sems.at[c]
            )
            for c in range(blocks.shape[0])
        ]
    )


def pick_kernel(index, source, target, sems):
    copy_all(
        [
            pltpu.make_async_copy(source.at[index[n]], target.at[n], sems.at[n])
            for n in range(target.shape[0])
        ]
    )


def pick_two_kernel(index, source, left, right, sems):
    count = left.shape[0]
    copy_all(
        [
            pltpu.make_async_copy(
                source.at[index[n], half], target.at[n], sems.at[half * count + n]
            )
            for half, target in ((1, right), (0, left))
            for n in range(count)
        ]
    )


def moved(kernel, index, operand, shapes, name, after=()):
    out = [jax.ShapeDtypeStruct(shape, operand.dtype) for shape in shapes]
    result = pl.pallas_call(
        kernel,
        out_shape=out,
        in_specs=[pl.BlockSpec(memory_space=pltpu.SMEM)]
        + [pl.BlockSpec(memory_space=pl.ANY)] * (1 + len(after)),
        out_specs=[pl.BlockSpec(memory_space=pl.ANY) for _ in out],
        scratch_shapes=[pltpu.SemaphoreType.DMA((len(out) * index.shape[0],))],
        compiler_params=pltpu.CompilerParams(vmem_limit_bytes=VMEM_LIMIT),
        name=name,
    )(index, operand, *after)
    return result if len(out) > 1 else result[0]


def pick(index, operand, name):
    return moved(pick_kernel, index, operand, [index.shape + operand.shape[1:]], name)


def pack_kernel(left, right, both, wide, sems):
    copies = []
    for half, source in enumerate((left, right)):
        for n in range(source.shape[0]):
            copies.append(
                pltpu.make_async_copy(source.at[n], wide.at[half, n], sems.at[half, n])
            )
            copies[-1].start()
    for n in range(left.shape[0]):
        for half in range(2):
            copies[half * left.shape[0] + n].wait()
            both[n, half] = wide[half, n].astype(jnp.bfloat16)


def pack(left, right):
    blocks = left.shape[0]
    return pl.pallas_call(
        pack_kernel,
        out_shape=jax.ShapeDtypeStruct((blocks, 2, BS, BS), jnp.bfloat16),
        in_specs=[pl.BlockSpec(memory_space=pl.ANY)] * 2,
        out_specs=pl.BlockSpec(memory_space=pltpu.VMEM),
        scratch_shapes=[
            pltpu.VMEM((2, blocks, BS, BS), jnp.float32),
            pltpu.SemaphoreType.DMA((2, blocks)),
        ],
        compiler_params=pltpu.CompilerParams(vmem_limit_bytes=VMEM_LIMIT),
        name="pack",
    )(left, right)


def split(value):
    high = value.astype(jnp.bfloat16)
    return high, (value - high.astype(jnp.float32)).astype(jnp.bfloat16)


def precondition_kernel(inverse_count, totals, lefts, rights, result):
    dot = functools.partial(jnp.dot, preferred_element_type=jnp.float32)
    for n in range(totals.shape[0]):
        grad = (totals[n].astype(jnp.float32) * inverse_count).astype(jnp.bfloat16)
        left, right = lefts[n], rights[n]
        high, low = split(dot(grad, right))
        precond = dot(left, high) + dot(left, low)
        wide = grad.astype(jnp.float32)
        scale = jnp.sqrt(jnp.mean(wide * wide) + EPS) / jnp.sqrt(
            jnp.mean(precond * precond) + EPS
        )
        result[n] = (precond * scale).astype(jnp.bfloat16)


def precondition(totals, lefts, rights, count):
    vmem = pl.BlockSpec(memory_space=pltpu.VMEM)
    return pl.pallas_call(
        functools.partial(precondition_kernel, 1.0 / count),
        out_shape=jax.ShapeDtypeStruct(totals.shape, jnp.bfloat16),
        in_specs=[vmem] * 3,
        out_specs=vmem,
        compiler_params=pltpu.CompilerParams(vmem_limit_bytes=VMEM_LIMIT),
        cost_estimate=pl.CostEstimate(
            flops=6 * totals.size * BS, bytes_accessed=8 * totals.size, transcendentals=0
        ),
        name="precondition",
    )(totals, lefts, rights)


def local(grads, owner_table, left_roots, right_roots):
    replicas = lax.axis_size("rep")
    groups = lax.axis_size("g")
    members = lax.axis_size("j")
    everywhere = ("rep", "g", "j")
    width = grads.shape[2]
    count = width // BS
    capacity = left_roots.shape[2]
    slots = members * capacity
    per_replica = count // replicas
    owners = owner_table.reshape(count)
    my_rep = lax.axis_index("rep")
    my_group = lax.axis_index("g")
    my_core = lax.axis_index("j") % 2
    order = jnp.arange(count, dtype=jnp.int32)

    packed = pack(
        left_roots.reshape(slots, BS, BS), right_roots.reshape(slots, BS, BS)
    )
    roots = lax.all_to_all(
        packed.reshape(members, capacity, 2, BS, BS), "j", split_axis=0, concat_axis=0, tiled=True
    ).reshape(slots, 2, BS, BS)

    before = (owners[None, :] < owners[:, None]) | (
        (owners[None, :] == owners[:, None]) & (order[None, :] < order[:, None])
    )
    place = jnp.sum(before.astype(jnp.int32), axis=1)
    stored = (place % replicas) * per_replica + place // replicas
    ordered = moved(
        place_kernel, stored, grads[0], [(count, BS, BS)], "place", (packed,)
    )
    total = lax.psum_scatter(ordered, "rep", scatter_dimension=0, tiled=True)

    sender = lax.ppermute(
        owner_table.reshape(1, count),
        ("rep", "g"),
        [(a * groups + b, b * groups + a) for a in range(replicas) for b in range(groups)],
    ).reshape(count)

    serves = jnp.asarray(REPLICA_AT)[my_core, :, my_rep]
    slot_owner = my_group * members + jnp.arange(members, dtype=jnp.int32)
    first = jnp.sum((sender[None, :] < slot_owner[:, None]).astype(jnp.int32), axis=1)
    named = jnp.sum((sender[None, :] == slot_owner[:, None]).astype(jnp.int32), axis=1)
    slot = jnp.arange(capacity, dtype=jnp.int32)
    slot_place = (first[:, None] + slot[None, :]).reshape(-1)
    slot_used = (slot[None, :] < named[:, None]).reshape(-1)
    taken = slot_used[None, :] & (slot_place[None, :] % replicas == serves[:, None])
    slot_order = jnp.arange(slots, dtype=jnp.int32)
    root_index = jnp.sum(jnp.where(taken, slot_order[None, :], 0), axis=1)

    sender_place = jnp.sum(
        (
            (sender[None, :] < sender[:, None])
            | ((sender[None, :] == sender[:, None]) & (order[None, :] < order[:, None]))
        ).astype(jnp.int32),
        axis=1,
    )
    held = serves[my_group] + replicas * jnp.arange(per_replica, dtype=jnp.int32)
    held_group = jnp.sum(
        jnp.where(sender_place[None, :] == held[:, None], sender[None, :], 0), axis=1
    ) // members

    def travel(half, name):
        half = lax.all_to_all(half, "g", split_axis=0, concat_axis=0, tiled=True)
        return lax.ppermute(pick(held_group, half, name), everywhere, along_rep())

    lefts, rights = moved(
        pick_two_kernel, root_index, roots, [(groups, BS, BS)] * 2, "pick_roots"
    )
    rights = travel(rights, "hold_right")
    lefts = travel(lefts, "hold_left")

    there = in_plane()
    totals = lax.ppermute(total, everywhere, there)
    outcome = precondition(totals, lefts, rights, replicas)
    mine = lax.ppermute(outcome, everywhere, [(b, a) for a, b in there])
    gathered = lax.all_gather(mine, "rep", axis=0, tiled=True)
    return moved(spread_kernel, stored, gathered, [(BS, width)], "spread")


def solution(mesh):
    replicas, shards = mesh.shape["rep"], mesh.shape["shard"]
    fine = Mesh(
        mesh.devices.reshape(replicas, shards // GROUP, GROUP), ("rep", "g", "j")
    )
    shard = ("g", "j")
    placed = (
        P("rep", shard, None),
        P(shard, None, None),
        P(shard, "rep", None, None, None),
        P(shard, "rep", None, None, None),
    )
    return jax.shard_map(
        local, mesh=fine, in_specs=placed, out_specs=P(shard, None), check_vma=False
    )
```

```python
import functools

import jax
import jax.numpy as jnp
import numpy as np
from jax import lax
from jax.experimental import pallas as pl
from jax.experimental.pallas import tpu as pltpu
from jax.sharding import PartitionSpec as P

BS = 256
EPS = 1e-06
REPLICAS = 8
SIDE = 4
GROUPS = 2 * SIDE
VMEM_LIMIT = 32 * 1024 * 1024


def device(group, member):
    core, a, b = group // SIDE, group // 2 % 2, group % 2
    x = 2 * a + member // 2 + (2 if core and member // 2 == 0 else 0)
    y = 2 * b + member % 2 + (2 if core and member % 2 == 0 else 0)
    return (x % SIDE * SIDE + y % SIDE) * 2 + core


MEMBERS = [[device(g, j) for j in range(SIDE)] for g in range(GROUPS)]
PEERS = [[device(g, j) for g in range(GROUPS)] for j in range(SIDE)]

STEPS = {
    "same": (0, 0),
    "half": (4, 4),
    "up": (2, 2),
    "down": (-2, -2),
    "up_a": (1, 3),
    "up_b": (3, 1),
    "down_a": (-1, -3),
    "down_b": (-3, -1),
}
COLUMNS = [
    ["down", "same", "up_a", "up_b", "down_b", "down_a", "half", "up"],
    ["up_a", "up_b", "same", "up", "half", "down", "down_a", "down_b"],
    ["up_b", "up_a", "same", "up", "down_a", "down_b", "down", "half"],
    ["up", "half", "up_b", "down_a", "down", "same", "down_b", "up_a"],
]
REPLICA_AT = np.array(
    [
        [[(m + STEPS[name][m % 2]) % REPLICAS for m in range(REPLICAS)] for name in names]
        for names in COLUMNS
    ],
    dtype=np.int32,
)


def along_rep():
    return [
        (
            m * SIDE * GROUPS + device(g, j),
            int(REPLICA_AT[j, g, m]) * SIDE * GROUPS + device(g, j),
        )
        for m in range(REPLICAS)
        for g in range(GROUPS)
        for j in range(SIDE)
    ]


def aside():
    return [
        (
            int(REPLICA_AT[j, g, m]) * SIDE * GROUPS + SIDE * m + j,
            int(REPLICA_AT[j, g, m]) * SIDE * GROUPS + device(g, j),
        )
        for m in range(REPLICAS)
        for g in range(GROUPS)
        for j in range(SIDE)
    ]


def announce():
    return [
        (g * SIDE * GROUPS + SIDE * m + j, m * SIDE * GROUPS + device(g, j))
        for m in range(REPLICAS)
        for g in range(GROUPS)
        for j in range(SIDE)
    ]


def copy_all(copies):
    for copy in copies:
        copy.start()
    for copy in copies:
        copy.wait()


def place_kernel(index, wide, *rest):
    blocks, sems = rest[-2:]
    copy_all(
        [
            pltpu.make_async_copy(
                wide.at[:, pl.ds(c * BS, BS)], blocks.at[index[c]], sems.at[c]
            )
            for c in range(blocks.shape[0])
        ]
    )


def spread_kernel(index, blocks, wide, sems):
    copy_all(
        [
            pltpu.make_async_copy(
                blocks.at[index[c]], wide.at[:, pl.ds(c * BS, BS)], sems.at[c]
            )
            for c in range(blocks.shape[0])
        ]
    )


def pick_kernel(index, source, target, sems):
    copy_all(
        [
            pltpu.make_async_copy(source.at[index[n]], target.at[n], sems.at[n])
            for n in range(target.shape[0])
        ]
    )


def pick_half_kernel(half, index, source, target, sems):
    copy_all(
        [
            pltpu.make_async_copy(source.at[index[n], half], target.at[n], sems.at[n])
            for n in range(target.shape[0])
        ]
    )


def moved(kernel, index, operand, shapes, name, after=()):
    out = [jax.ShapeDtypeStruct(shape, operand.dtype) for shape in shapes]
    result = pl.pallas_call(
        kernel,
        out_shape=out,
        in_specs=[pl.BlockSpec(memory_space=pltpu.SMEM)]
        + [pl.BlockSpec(memory_space=pl.ANY)] * (1 + len(after)),
        out_specs=[pl.BlockSpec(memory_space=pl.ANY) for _ in out],
        scratch_shapes=[pltpu.SemaphoreType.DMA((len(out) * index.shape[0],))],
        compiler_params=pltpu.CompilerParams(vmem_limit_bytes=VMEM_LIMIT),
        name=name,
    )(index, operand, *after)
    return result if len(out) > 1 else result[0]


def pick(index, operand, name):
    return moved(pick_kernel, index, operand, [index.shape + operand.shape[1:]], name)


def pack_kernel(left, right, both):
    for n in range(left.shape[0]):
        both[n, 0] = left[n].astype(jnp.bfloat16)
        both[n, 1] = right[n].astype(jnp.bfloat16)


def pack(left, right):
    vmem = pl.BlockSpec(memory_space=pltpu.VMEM)
    return pl.pallas_call(
        pack_kernel,
        out_shape=jax.ShapeDtypeStruct((left.shape[0], 2, BS, BS), jnp.bfloat16),
        in_specs=[vmem] * 2,
        out_specs=vmem,
        compiler_params=pltpu.CompilerParams(vmem_limit_bytes=VMEM_LIMIT),
        name="pack",
    )(left, right)


def split(value):
    high = value.astype(jnp.bfloat16)
    return high, (value - high.astype(jnp.float32)).astype(jnp.bfloat16)


def precondition_kernel(inverse_count, totals, lefts, rights, result):
    dot = functools.partial(jnp.dot, preferred_element_type=jnp.float32)
    for n in range(totals.shape[0]):
        grad = (totals[n].astype(jnp.float32) * inverse_count).astype(jnp.bfloat16)
        left, right = lefts[n], rights[n]
        high, low = split(dot(grad, right))
        precond = dot(left, high) + dot(left, low)
        wide = grad.astype(jnp.float32)
        scale = jnp.sqrt(jnp.mean(wide * wide) + EPS) / jnp.sqrt(
            jnp.mean(precond * precond) + EPS
        )
        result[n] = (precond * scale).astype(jnp.bfloat16)


def precondition(totals, lefts, rights, count):
    vmem = pl.BlockSpec(memory_space=pltpu.VMEM)
    return pl.pallas_call(
        functools.partial(precondition_kernel, 1.0 / count),
        out_shape=jax.ShapeDtypeStruct(totals.shape, jnp.bfloat16),
        in_specs=[vmem] * 3,
        out_specs=vmem,
        compiler_params=pltpu.CompilerParams(vmem_limit_bytes=VMEM_LIMIT),
        cost_estimate=pl.CostEstimate(
            flops=6 * totals.size * BS, bytes_accessed=8 * totals.size, transcendentals=0
        ),
        name="precondition",
    )(totals, lefts, rights)


def place_of(keys):
    order = jnp.arange(keys.shape[0], dtype=jnp.int32)
    before = (keys[None, :] < keys[:, None]) | (
        (keys[None, :] == keys[:, None]) & (order[None, :] < order[:, None])
    )
    return jnp.sum(before.astype(jnp.int32), axis=1)


def group_and_member(index):
    x, y, core = index // (2 * SIDE), index // 2 % SIDE, index % 2
    a, b = (x - core) % SIDE // 2, (y - core) % SIDE // 2
    return core * SIDE + a * 2 + b, x % 2 * 2 + y % 2


def key_of(owners):
    group, member = group_and_member(owners)
    return group * SIDE + member


def local(grads, owner_table, left_roots, right_roots):
    replicas = lax.axis_size("rep")
    everywhere = ("rep", "shard")
    width = grads.shape[2]
    count = width // BS
    capacity = left_roots.shape[2]
    slots = SIDE * capacity
    per_replica = count // replicas
    my_rep = lax.axis_index("rep")
    my_group, my_member = group_and_member(lax.axis_index("shard"))

    keys = key_of(owner_table.reshape(count))
    place = place_of(keys)
    stored = (place % replicas) * per_replica + place // replicas

    packed = pack(
        left_roots.reshape(slots, BS, BS), right_roots.reshape(slots, BS, BS)
    )
    roots = lax.all_to_all(
        packed.reshape(SIDE, capacity, 2, BS, BS),
        "shard",
        split_axis=0,
        concat_axis=0,
        axis_index_groups=MEMBERS,
        tiled=True,
    ).reshape(slots, 2, BS, BS)
    ordered = moved(place_kernel, stored, grads[0], [(count, BS, BS)], "place", (packed,))
    total = lax.psum_scatter(ordered, "rep", scatter_dimension=0, tiled=True)

    told = lax.ppermute(jnp.stack([keys, place]), everywhere, announce())
    sender_key, sender_place = told[0], told[1]
    serves = jnp.asarray(REPLICA_AT)[my_member, :, my_rep]
    slot_key = my_group * SIDE + jnp.arange(SIDE, dtype=jnp.int32)
    first = jnp.sum((sender_key[None, :] < slot_key[:, None]).astype(jnp.int32), axis=1)
    named = jnp.sum((sender_key[None, :] == slot_key[:, None]).astype(jnp.int32), axis=1)
    slot = jnp.arange(capacity, dtype=jnp.int32)
    slot_place = (first[:, None] + slot[None, :]).reshape(-1)
    slot_used = (slot[None, :] < named[:, None]).reshape(-1)
    taken = slot_used[None, :] & (slot_place[None, :] % replicas == serves[:, None])
    slot_order = jnp.arange(slots, dtype=jnp.int32)
    root_index = jnp.sum(jnp.where(taken, slot_order[None, :], 0), axis=1)

    held = serves[my_group] + replicas * jnp.arange(per_replica, dtype=jnp.int32)
    held_group = jnp.sum(
        jnp.where(sender_place[None, :] == held[:, None], sender_key[None, :], 0),
        axis=1,
    ) // SIDE

    def sort_out(half, name):
        half = moved(
            functools.partial(pick_half_kernel, half), root_index, roots, [(GROUPS, BS, BS)], name
        )
        return lax.all_to_all(
            half, "shard", split_axis=0, concat_axis=0, axis_index_groups=PEERS, tiled=True
        )

    rights, lefts = sort_out(1, "pick_right"), sort_out(0, "pick_left")
    there = aside()
    total = lax.ppermute(total, everywhere, there)
    rights = lax.ppermute(pick(held_group, rights, "hold_right"), everywhere, along_rep())
    lefts = lax.ppermute(pick(held_group, lefts, "hold_left"), everywhere, along_rep())
    outcome = precondition(total, lefts, rights, replicas)
    mine = lax.ppermute(outcome, everywhere, [(b, a) for a, b in there])
    gathered = lax.all_gather(mine, "rep", axis=0, tiled=True)
    return moved(spread_kernel, stored, gathered, [(BS, width)], "spread")


def solution(mesh):
    placed = (
        P("rep", "shard", None),
        P("shard", None, None),
        P("shard", "rep", None, None, None),
        P("shard", "rep", None, None, None),
    )
    return jax.shard_map(
        local, mesh=mesh, in_specs=placed, out_specs=P("shard", None), check_vma=False
    )
```

```python
import functools

import jax
import jax.numpy as jnp
import numpy as np
from jax import lax
from jax.experimental import pallas as pl
from jax.experimental.pallas import tpu as pltpu
from jax.sharding import PartitionSpec as P

BS = 256
EPS = 1e-06
REPLICAS = 8
SIDE = 4
GROUPS = 2 * SIDE
VMEM_LIMIT = 32 * 1024 * 1024


def device(group, member):
    core, a, b = group // SIDE, group // 2 % 2, group % 2
    x = 2 * a + member // 2 + (2 if core and member // 2 == 0 else 0)
    y = 2 * b + member % 2 + (2 if core and member % 2 == 0 else 0)
    return (x % SIDE * SIDE + y % SIDE) * 2 + core


MEMBERS = [[device(g, j) for j in range(SIDE)] for g in range(GROUPS)]
PEERS = [[device(g, j) for g in range(GROUPS)] for j in range(SIDE)]

STEPS = {
    "same": (0, 0),
    "half": (4, 4),
    "up": (2, 2),
    "down": (-2, -2),
    "up_a": (1, 3),
    "up_b": (3, 1),
    "down_a": (-1, -3),
    "down_b": (-3, -1),
}
COLUMNS = [
    ["down", "same", "up_a", "up_b", "down_b", "down_a", "half", "up"],
    ["up_a", "up_b", "same", "up", "half", "down", "down_a", "down_b"],
    ["up_b", "up_a", "same", "up", "down_a", "down_b", "down", "half"],
    ["up", "half", "up_b", "down_a", "down", "same", "down_b", "up_a"],
]
REPLICA_AT = np.array(
    [
        [[(m + STEPS[name][m % 2]) % REPLICAS for m in range(REPLICAS)] for name in names]
        for names in COLUMNS
    ],
    dtype=np.int32,
)


def along_rep():
    return [
        (
            m * SIDE * GROUPS + device(g, j),
            int(REPLICA_AT[j, g, m]) * SIDE * GROUPS + device(g, j),
        )
        for m in range(REPLICAS)
        for g in range(GROUPS)
        for j in range(SIDE)
    ]


def aside():
    return [
        (
            int(REPLICA_AT[j, g, m]) * SIDE * GROUPS + SIDE * m + j,
            int(REPLICA_AT[j, g, m]) * SIDE * GROUPS + device(g, j),
        )
        for m in range(REPLICAS)
        for g in range(GROUPS)
        for j in range(SIDE)
    ]


def announce():
    return [
        (g * SIDE * GROUPS + SIDE * m + j, m * SIDE * GROUPS + device(g, j))
        for m in range(REPLICAS)
        for g in range(GROUPS)
        for j in range(SIDE)
    ]


def copy_all(copies):
    for copy in copies:
        copy.start()
    for copy in copies:
        copy.wait()


def place_kernel(index, wide, *rest):
    blocks, sems = rest[-2:]
    copy_all(
        [
            pltpu.make_async_copy(
                wide.at[:, pl.ds(c * BS, BS)], blocks.at[index[c]], sems.at[c]
            )
            for c in range(blocks.shape[0])
        ]
    )


def spread_kernel(index, blocks, wide, sems):
    copy_all(
        [
            pltpu.make_async_copy(
                blocks.at[index[c]], wide.at[:, pl.ds(c * BS, BS)], sems.at[c]
            )
            for c in range(blocks.shape[0])
        ]
    )


def pick_kernel(index, source, target, sems):
    copy_all(
        [
            pltpu.make_async_copy(source.at[index[n]], target.at[n], sems.at[n])
            for n in range(target.shape[0])
        ]
    )


def moved(kernel, index, operand, shapes, name, after=()):
    out = [jax.ShapeDtypeStruct(shape, operand.dtype) for shape in shapes]
    result = pl.pallas_call(
        kernel,
        out_shape=out,
        in_specs=[pl.BlockSpec(memory_space=pltpu.SMEM)]
        + [pl.BlockSpec(memory_space=pl.ANY)] * (1 + len(after)),
        out_specs=[pl.BlockSpec(memory_space=pl.ANY) for _ in out],
        scratch_shapes=[pltpu.SemaphoreType.DMA((len(out) * index.shape[0],))],
        compiler_params=pltpu.CompilerParams(vmem_limit_bytes=VMEM_LIMIT),
        name=name,
    )(index, operand, *after)
    return result if len(out) > 1 else result[0]


def pick(index, operand, name):
    return moved(pick_kernel, index, operand, [index.shape + operand.shape[1:]], name)


def pack_kernel(left, right, both):
    for n in range(left.shape[0]):
        both[n, 0] = left[n].astype(jnp.bfloat16)
        both[n, 1] = right[n].astype(jnp.bfloat16)


def pack(left, right):
    vmem = pl.BlockSpec(memory_space=pltpu.VMEM)
    return pl.pallas_call(
        pack_kernel,
        out_shape=jax.ShapeDtypeStruct((left.shape[0], 2, BS, BS), jnp.bfloat16),
        in_specs=[vmem] * 2,
        out_specs=vmem,
        compiler_params=pltpu.CompilerParams(vmem_limit_bytes=VMEM_LIMIT),
        name="pack",
    )(left, right)


def split(value):
    high = value.astype(jnp.bfloat16)
    return high, (value - high.astype(jnp.float32)).astype(jnp.bfloat16)


def precondition_kernel(inverse_count, totals, roots, result):
    dot = functools.partial(jnp.dot, preferred_element_type=jnp.float32)
    for n in range(totals.shape[0]):
        grad = (totals[n].astype(jnp.float32) * inverse_count).astype(jnp.bfloat16)
        left, right = roots[n, 0], roots[n, 1]
        high, low = split(dot(grad, right))
        precond = dot(left, high) + dot(left, low)
        wide = grad.astype(jnp.float32)
        scale = jnp.sqrt(jnp.mean(wide * wide) + EPS) / jnp.sqrt(
            jnp.mean(precond * precond) + EPS
        )
        result[n] = (precond * scale).astype(jnp.bfloat16)


def precondition(totals, roots, count):
    vmem = pl.BlockSpec(memory_space=pltpu.VMEM)
    return pl.pallas_call(
        functools.partial(precondition_kernel, 1.0 / count),
        out_shape=jax.ShapeDtypeStruct(totals.shape, jnp.bfloat16),
        in_specs=[vmem] * 2,
        out_specs=vmem,
        compiler_params=pltpu.CompilerParams(vmem_limit_bytes=VMEM_LIMIT),
        cost_estimate=pl.CostEstimate(
            flops=6 * totals.size * BS, bytes_accessed=8 * totals.size, transcendentals=0
        ),
        name="precondition",
    )(totals, roots)


def place_of(keys):
    order = jnp.arange(keys.shape[0], dtype=jnp.int32)
    before = (keys[None, :] < keys[:, None]) | (
        (keys[None, :] == keys[:, None]) & (order[None, :] < order[:, None])
    )
    return jnp.sum(before.astype(jnp.int32), axis=1)


def group_and_member(index):
    x, y, core = index // (2 * SIDE), index // 2 % SIDE, index % 2
    a, b = (x - core) % SIDE // 2, (y - core) % SIDE // 2
    return core * SIDE + a * 2 + b, x % 2 * 2 + y % 2


def key_of(owners):
    group, member = group_and_member(owners)
    return group * SIDE + member


def local(grads, owner_table, left_roots, right_roots):
    replicas = lax.axis_size("rep")
    everywhere = ("rep", "shard")
    width = grads.shape[2]
    count = width // BS
    capacity = left_roots.shape[2]
    slots = SIDE * capacity
    per_replica = count // replicas
    my_rep = lax.axis_index("rep")
    my_group, my_member = group_and_member(lax.axis_index("shard"))

    keys = key_of(owner_table.reshape(count))
    place = place_of(keys)
    stored = (place % replicas) * per_replica + place // replicas

    packed = pack(
        left_roots.reshape(slots, BS, BS), right_roots.reshape(slots, BS, BS)
    )
    roots = lax.all_to_all(
        packed.reshape(SIDE, capacity, 2, BS, BS),
        "shard",
        split_axis=0,
        concat_axis=0,
        axis_index_groups=MEMBERS,
        tiled=True,
    ).reshape(slots, 2, BS, BS)
    ordered = moved(place_kernel, stored, grads[0], [(count, BS, BS)], "place", (packed,))
    total = lax.psum_scatter(ordered, "rep", scatter_dimension=0, tiled=True)

    told = lax.ppermute(jnp.stack([keys, place]), everywhere, announce())
    sender_key, sender_place = told[0], told[1]
    serves = jnp.asarray(REPLICA_AT)[my_member, :, my_rep]
    slot_key = my_group * SIDE + jnp.arange(SIDE, dtype=jnp.int32)
    first = jnp.sum((sender_key[None, :] < slot_key[:, None]).astype(jnp.int32), axis=1)
    named = jnp.sum((sender_key[None, :] == slot_key[:, None]).astype(jnp.int32), axis=1)
    slot = jnp.arange(capacity, dtype=jnp.int32)
    slot_place = (first[:, None] + slot[None, :]).reshape(-1)
    slot_used = (slot[None, :] < named[:, None]).reshape(-1)
    taken = slot_used[None, :] & (slot_place[None, :] % replicas == serves[:, None])
    slot_order = jnp.arange(slots, dtype=jnp.int32)
    root_index = jnp.sum(jnp.where(taken, slot_order[None, :], 0), axis=1)

    held = serves[my_group] + replicas * jnp.arange(per_replica, dtype=jnp.int32)
    held_group = jnp.sum(
        jnp.where(sender_place[None, :] == held[:, None], sender_key[None, :], 0),
        axis=1,
    ) // SIDE

    roots = lax.all_to_all(
        pick(root_index, roots, "pick_roots"),
        "shard",
        split_axis=0,
        concat_axis=0,
        axis_index_groups=PEERS,
        tiled=True,
    )
    roots = pick(held_group, roots, "hold_roots")
    back = {b: a for a, b in aside()}
    roots = lax.ppermute(roots, everywhere, [(a, back[b]) for a, b in along_rep()])
    mine = precondition(total, roots, replicas)
    gathered = lax.all_gather(mine, "rep", axis=0, tiled=True)
    return moved(spread_kernel, stored, gathered, [(BS, width)], "spread")


def solution(mesh):
    placed = (
        P("rep", "shard", None),
        P("shard", None, None),
        P("shard", "rep", None, None, None),
        P("shard", "rep", None, None, None),
    )
    return jax.shard_map(
        local, mesh=mesh, in_specs=placed, out_specs=P("shard", None), check_vma=False
    )
```

```python
import functools

import jax
import jax.numpy as jnp
import numpy as np
from jax import lax
from jax.experimental import pallas as pl
from jax.experimental.pallas import tpu as pltpu
from jax.sharding import PartitionSpec as P

BS = 256
EPS = 1e-06
REPLICAS = 8
SIDE = 4
GROUPS = 2 * SIDE
VMEM_LIMIT = 32 * 1024 * 1024


def device(group, member):
    core, a, b = group // SIDE, group // 2 % 2, group % 2
    x = 2 * a + member // 2 + (2 if core and member // 2 == 0 else 0)
    y = 2 * b + member % 2 + (2 if core and member % 2 == 0 else 0)
    return (x % SIDE * SIDE + y % SIDE) * 2 + core


MEMBERS = [[device(g, j) for j in range(SIDE)] for g in range(GROUPS)]
PEERS = [[device(g, j) for g in range(GROUPS)] for j in range(SIDE)]

STEPS = {
    "same": (0, 0),
    "half": (4, 4),
    "up": (2, 2),
    "down": (-2, -2),
    "up_a": (1, 3),
    "up_b": (3, 1),
    "down_a": (-1, -3),
    "down_b": (-3, -1),
}
COLUMNS = [
    ["up", "same", "up_b", "up_a", "down_a", "down_b", "half", "down"],
    ["same", "up", "up_a", "up_b", "down_a", "down_b", "half", "down"],
    ["same", "up", "down_a", "up_b", "down", "half", "down_b", "up_a"],
    ["up", "half", "up_b", "down_a", "down", "same", "down_b", "up_a"],
]
REPLICA_AT = np.array(
    [
        [[(m + STEPS[name][m % 2]) % REPLICAS for m in range(REPLICAS)] for name in names]
        for names in COLUMNS
    ],
    dtype=np.int32,
)


def along_rep():
    return [
        (
            m * SIDE * GROUPS + device(g, j),
            int(REPLICA_AT[j, g, m]) * SIDE * GROUPS + device(g, j),
        )
        for m in range(REPLICAS)
        for g in range(GROUPS)
        for j in range(SIDE)
    ]


def aside():
    return [
        (
            int(REPLICA_AT[j, g, m]) * SIDE * GROUPS + SIDE * m + j,
            int(REPLICA_AT[j, g, m]) * SIDE * GROUPS + device(g, j),
        )
        for m in range(REPLICAS)
        for g in range(GROUPS)
        for j in range(SIDE)
    ]


def announce():
    return [
        (g * SIDE * GROUPS + SIDE * m + j, m * SIDE * GROUPS + device(g, j))
        for m in range(REPLICAS)
        for g in range(GROUPS)
        for j in range(SIDE)
    ]


def copy_all(copies):
    for copy in copies:
        copy.start()
    for copy in copies:
        copy.wait()


def place_kernel(index, wide, *rest):
    blocks, sems = rest[-2:]
    copy_all(
        [
            pltpu.make_async_copy(
                wide.at[:, pl.ds(c * BS, BS)], blocks.at[index[c]], sems.at[c]
            )
            for c in range(blocks.shape[0])
        ]
    )


def spread_kernel(index, blocks, wide, sems):
    copy_all(
        [
            pltpu.make_async_copy(
                blocks.at[index[c]], wide.at[:, pl.ds(c * BS, BS)], sems.at[c]
            )
            for c in range(blocks.shape[0])
        ]
    )


def pick_kernel(index, source, target, sems):
    copy_all(
        [
            pltpu.make_async_copy(source.at[index[n]], target.at[n], sems.at[n])
            for n in range(target.shape[0])
        ]
    )


def moved(kernel, index, operand, shapes, name, after=()):
    out = [jax.ShapeDtypeStruct(shape, operand.dtype) for shape in shapes]
    result = pl.pallas_call(
        kernel,
        out_shape=out,
        in_specs=[pl.BlockSpec(memory_space=pltpu.SMEM)]
        + [pl.BlockSpec(memory_space=pl.ANY)] * (1 + len(after)),
        out_specs=[pl.BlockSpec(memory_space=pl.ANY) for _ in out],
        scratch_shapes=[pltpu.SemaphoreType.DMA((len(out) * index.shape[0],))],
        compiler_params=pltpu.CompilerParams(vmem_limit_bytes=VMEM_LIMIT),
        name=name,
    )(index, operand, *after)
    return result if len(out) > 1 else result[0]


def pick(index, operand, name):
    return moved(pick_kernel, index, operand, [index.shape + operand.shape[1:]], name)


def pack_kernel(left, right, both):
    for n in range(left.shape[0]):
        both[n, 0] = left[n].astype(jnp.bfloat16)
        both[n, 1] = right[n].astype(jnp.bfloat16)


def pack(left, right):
    vmem = pl.BlockSpec(memory_space=pltpu.VMEM)
    return pl.pallas_call(
        pack_kernel,
        out_shape=jax.ShapeDtypeStruct((left.shape[0], 2, BS, BS), jnp.bfloat16),
        in_specs=[vmem] * 2,
        out_specs=vmem,
        compiler_params=pltpu.CompilerParams(vmem_limit_bytes=VMEM_LIMIT),
        name="pack",
    )(left, right)


def split(value):
    high = value.astype(jnp.bfloat16)
    return high, (value - high.astype(jnp.float32)).astype(jnp.bfloat16)


def precondition_kernel(inverse_count, totals, roots, result):
    dot = functools.partial(jnp.dot, preferred_element_type=jnp.float32)
    for n in range(totals.shape[0]):
        grad = (totals[n].astype(jnp.float32) * inverse_count).astype(jnp.bfloat16)
        left, right = roots[n, 0], roots[n, 1]
        high, low = split(dot(grad, right))
        precond = dot(left, high) + dot(left, low)
        wide = grad.astype(jnp.float32)
        scale = jnp.sqrt(jnp.mean(wide * wide) + EPS) / jnp.sqrt(
            jnp.mean(precond * precond) + EPS
        )
        result[n] = (precond * scale).astype(jnp.bfloat16)


def precondition(totals, roots, count):
    vmem = pl.BlockSpec(memory_space=pltpu.VMEM)
    return pl.pallas_call(
        functools.partial(precondition_kernel, 1.0 / count),
        out_shape=jax.ShapeDtypeStruct(totals.shape, jnp.bfloat16),
        in_specs=[vmem] * 2,
        out_specs=vmem,
        compiler_params=pltpu.CompilerParams(vmem_limit_bytes=VMEM_LIMIT),
        cost_estimate=pl.CostEstimate(
            flops=6 * totals.size * BS, bytes_accessed=8 * totals.size, transcendentals=0
        ),
        name="precondition",
    )(totals, roots)


def place_of(keys):
    order = jnp.arange(keys.shape[0], dtype=jnp.int32)
    before = (keys[None, :] < keys[:, None]) | (
        (keys[None, :] == keys[:, None]) & (order[None, :] < order[:, None])
    )
    return jnp.sum(before.astype(jnp.int32), axis=1)


def group_and_member(index):
    x, y, core = index // (2 * SIDE), index // 2 % SIDE, index % 2
    a, b = (x - core) % SIDE // 2, (y - core) % SIDE // 2
    return core * SIDE + a * 2 + b, x % 2 * 2 + y % 2


def key_of(owners):
    group, member = group_and_member(owners)
    return group * SIDE + member


def local(grads, owner_table, left_roots, right_roots):
    replicas = lax.axis_size("rep")
    everywhere = ("rep", "shard")
    width = grads.shape[2]
    count = width // BS
    capacity = left_roots.shape[2]
    slots = SIDE * capacity
    per_replica = count // replicas
    my_rep = lax.axis_index("rep")
    my_group, my_member = group_and_member(lax.axis_index("shard"))

    keys = key_of(owner_table.reshape(count))
    place = place_of(keys)
    stored = (place % replicas) * per_replica + place // replicas

    packed = pack(
        left_roots.reshape(slots, BS, BS), right_roots.reshape(slots, BS, BS)
    )
    roots = lax.all_to_all(
        packed.reshape(SIDE, capacity, 2, BS, BS),
        "shard",
        split_axis=0,
        concat_axis=0,
        axis_index_groups=MEMBERS,
        tiled=True,
    ).reshape(slots, 2, BS, BS)
    ordered = moved(place_kernel, stored, grads[0], [(count, BS, BS)], "place", (packed,))
    total = lax.psum_scatter(ordered, "rep", scatter_dimension=0, tiled=True)

    told = lax.ppermute(jnp.stack([keys, place]), everywhere, announce())
    sender_key, sender_place = told[0], told[1]
    serves = jnp.asarray(REPLICA_AT)[my_member, :, my_rep]
    slot_key = my_group * SIDE + jnp.arange(SIDE, dtype=jnp.int32)
    first = jnp.sum((sender_key[None, :] < slot_key[:, None]).astype(jnp.int32), axis=1)
    named = jnp.sum((sender_key[None, :] == slot_key[:, None]).astype(jnp.int32), axis=1)
    slot = jnp.arange(capacity, dtype=jnp.int32)
    slot_place = (first[:, None] + slot[None, :]).reshape(-1)
    slot_used = (slot[None, :] < named[:, None]).reshape(-1)
    taken = slot_used[None, :] & (slot_place[None, :] % replicas == serves[:, None])
    slot_order = jnp.arange(slots, dtype=jnp.int32)
    root_index = jnp.sum(jnp.where(taken, slot_order[None, :], 0), axis=1)

    held = serves[my_group] + replicas * jnp.arange(per_replica, dtype=jnp.int32)
    held_group = jnp.sum(
        jnp.where(sender_place[None, :] == held[:, None], sender_key[None, :], 0),
        axis=1,
    ) // SIDE

    roots = lax.all_to_all(
        pick(root_index, roots, "pick_roots"),
        "shard",
        split_axis=0,
        concat_axis=0,
        axis_index_groups=PEERS,
        tiled=True,
    )
    roots = pick(held_group, roots, "hold_roots")
    back = {b: a for a, b in aside()}
    roots = lax.ppermute(roots, everywhere, [(a, back[b]) for a, b in along_rep()])
    mine = precondition(total, roots, replicas)
    gathered = lax.all_gather(mine, "rep", axis=0, tiled=True)
    return moved(spread_kernel, stored, gathered, [(BS, width)], "spread")


def solution(mesh):
    placed = (
        P("rep", "shard", None),
        P("shard", None, None),
        P("shard", "rep", None, None, None),
        P("shard", "rep", None, None, None),
    )
    return jax.shard_map(
        local, mesh=mesh, in_specs=placed, out_specs=P("shard", None), check_vma=False
    )
```

```python
import functools

import jax
import jax.numpy as jnp
import numpy as np
from jax import lax
from jax.experimental import pallas as pl
from jax.experimental.pallas import tpu as pltpu
from jax.sharding import PartitionSpec as P

BS = 256
EPS = 1e-06
REPLICAS = 8
SIDE = 4
GROUPS = 2 * SIDE
VMEM_LIMIT = 32 * 1024 * 1024


def device(group, member):
    core, a, b = group // SIDE, group // 2 % 2, group % 2
    x = 2 * a + member // 2 + (2 if core and member // 2 == 0 else 0)
    y = 2 * b + member % 2 + (2 if core and member % 2 == 0 else 0)
    return (x % SIDE * SIDE + y % SIDE) * 2 + core


MEMBERS = [[device(g, j) for j in range(SIDE)] for g in range(GROUPS)]
PEERS = [[device(g, j) for g in range(GROUPS)] for j in range(SIDE)]

STEPS = {
    "same": (0, 0),
    "half": (4, 4),
    "up": (2, 2),
    "down": (-2, -2),
    "up_a": (1, 3),
    "up_b": (3, 1),
    "down_a": (-1, -3),
    "down_b": (-3, -1),
}
COLUMNS = [
    ["up", "same", "up_b", "up_a", "down_a", "down_b", "half", "down"],
    ["same", "up", "up_a", "up_b", "down_a", "down_b", "half", "down"],
    ["same", "up", "down_a", "up_b", "down", "half", "down_b", "up_a"],
    ["up", "half", "up_b", "down_a", "down", "same", "down_b", "up_a"],
]
REPLICA_AT = np.array(
    [
        [[(m + STEPS[name][m % 2]) % REPLICAS for m in range(REPLICAS)] for name in names]
        for names in COLUMNS
    ],
    dtype=np.int32,
)


def along_rep():
    return [
        (
            m * SIDE * GROUPS + device(g, j),
            int(REPLICA_AT[j, g, m]) * SIDE * GROUPS + device(g, j),
        )
        for m in range(REPLICAS)
        for g in range(GROUPS)
        for j in range(SIDE)
    ]


def aside():
    return [
        (
            int(REPLICA_AT[j, g, m]) * SIDE * GROUPS + SIDE * m + j,
            int(REPLICA_AT[j, g, m]) * SIDE * GROUPS + device(g, j),
        )
        for m in range(REPLICAS)
        for g in range(GROUPS)
        for j in range(SIDE)
    ]


def announce():
    return [
        (g * SIDE * GROUPS + SIDE * m + j, m * SIDE * GROUPS + device(g, j))
        for m in range(REPLICAS)
        for g in range(GROUPS)
        for j in range(SIDE)
    ]


def copy_all(copies):
    for copy in copies:
        copy.start()
    for copy in copies:
        copy.wait()


def place_kernel(index, wide, *rest):
    blocks, sems = rest[-2:]
    copy_all(
        [
            pltpu.make_async_copy(
                wide.at[:, pl.ds(c * BS, BS)], blocks.at[index[c]], sems.at[c]
            )
            for c in range(blocks.shape[0])
        ]
    )


def spread_kernel(index, blocks, wide, sems):
    copy_all(
        [
            pltpu.make_async_copy(
                blocks.at[index[c]], wide.at[:, pl.ds(c * BS, BS)], sems.at[c]
            )
            for c in range(blocks.shape[0])
        ]
    )


def pick_kernel(index, source, target, sems):
    copy_all(
        [
            pltpu.make_async_copy(source.at[index[n]], target.at[n], sems.at[n])
            for n in range(target.shape[0])
        ]
    )


def moved(kernel, index, operand, shapes, name, after=()):
    out = [jax.ShapeDtypeStruct(shape, operand.dtype) for shape in shapes]
    result = pl.pallas_call(
        kernel,
        out_shape=out,
        in_specs=[pl.BlockSpec(memory_space=pltpu.SMEM)]
        + [pl.BlockSpec(memory_space=pl.ANY)] * (1 + len(after)),
        out_specs=[pl.BlockSpec(memory_space=pl.ANY) for _ in out],
        scratch_shapes=[pltpu.SemaphoreType.DMA((len(out) * index.shape[0],))],
        compiler_params=pltpu.CompilerParams(vmem_limit_bytes=VMEM_LIMIT),
        name=name,
    )(index, operand, *after)
    return result if len(out) > 1 else result[0]


def pick(index, operand, name):
    return moved(pick_kernel, index, operand, [index.shape + operand.shape[1:]], name)


def pack_kernel(left, right, both):
    for n in range(left.shape[0]):
        both[n, 0] = left[n].astype(jnp.bfloat16)
        both[n, 1] = right[n].astype(jnp.bfloat16)


def pack(left, right):
    vmem = pl.BlockSpec(memory_space=pltpu.VMEM)
    return pl.pallas_call(
        pack_kernel,
        out_shape=jax.ShapeDtypeStruct((left.shape[0], 2, BS, BS), jnp.bfloat16),
        in_specs=[vmem] * 2,
        out_specs=vmem,
        compiler_params=pltpu.CompilerParams(vmem_limit_bytes=VMEM_LIMIT),
        name="pack",
    )(left, right)


def split(value):
    high = value.astype(jnp.bfloat16)
    return high, (value - high.astype(jnp.float32)).astype(jnp.bfloat16)


def prepare_kernel(inverse_count, totals, means, sizes):
    for n in range(totals.shape[0]):
        mean = (totals[n].astype(jnp.float32) * inverse_count).astype(jnp.bfloat16)
        wide = mean.astype(jnp.float32)
        means[n] = mean
        sizes[n] = jnp.sqrt(jnp.mean(wide * wide) + EPS)


def prepare(totals, count):
    vmem = pl.BlockSpec(memory_space=pltpu.VMEM)
    return pl.pallas_call(
        functools.partial(prepare_kernel, 1.0 / count),
        out_shape=[
            jax.ShapeDtypeStruct(totals.shape, jnp.bfloat16),
            jax.ShapeDtypeStruct(totals.shape[:1], jnp.float32),
        ],
        in_specs=[vmem],
        out_specs=[vmem, pl.BlockSpec(memory_space=pltpu.SMEM)],
        compiler_params=pltpu.CompilerParams(vmem_limit_bytes=VMEM_LIMIT),
        cost_estimate=pl.CostEstimate(
            flops=64 * totals.size, bytes_accessed=8 * totals.size, transcendentals=0
        ),
        name="prepare",
    )(totals)


def precondition_kernel(sizes, means, roots, result):
    dot = functools.partial(jnp.dot, preferred_element_type=jnp.float32)
    for n in range(means.shape[0]):
        left, right = roots[n, 0], roots[n, 1]
        high, low = split(dot(means[n], right))
        precond = dot(left, high) + dot(left, low)
        scale = sizes[n] / jnp.sqrt(jnp.mean(precond * precond) + EPS)
        result[n] = (precond * scale).astype(jnp.bfloat16)


def precondition(means, sizes, roots):
    vmem = pl.BlockSpec(memory_space=pltpu.VMEM)
    return pl.pallas_call(
        precondition_kernel,
        out_shape=jax.ShapeDtypeStruct(means.shape, jnp.bfloat16),
        in_specs=[pl.BlockSpec(memory_space=pltpu.SMEM), vmem, vmem],
        out_specs=vmem,
        compiler_params=pltpu.CompilerParams(vmem_limit_bytes=VMEM_LIMIT),
        cost_estimate=pl.CostEstimate(
            flops=6 * means.size * BS, bytes_accessed=8 * means.size, transcendentals=0
        ),
        name="precondition",
    )(sizes, means, roots)


def place_of(keys):
    order = jnp.arange(keys.shape[0], dtype=jnp.int32)
    before = (keys[None, :] < keys[:, None]) | (
        (keys[None, :] == keys[:, None]) & (order[None, :] < order[:, None])
    )
    return jnp.sum(before.astype(jnp.int32), axis=1)


def group_and_member(index):
    x, y, core = index // (2 * SIDE), index // 2 % SIDE, index % 2
    a, b = (x - core) % SIDE // 2, (y - core) % SIDE // 2
    return core * SIDE + a * 2 + b, x % 2 * 2 + y % 2


def key_of(owners):
    group, member = group_and_member(owners)
    return group * SIDE + member


def local(grads, owner_table, left_roots, right_roots):
    replicas = lax.axis_size("rep")
    everywhere = ("rep", "shard")
    width = grads.shape[2]
    count = width // BS
    capacity = left_roots.shape[2]
    slots = SIDE * capacity
    per_replica = count // replicas
    my_rep = lax.axis_index("rep")
    my_group, my_member = group_and_member(lax.axis_index("shard"))

    keys = key_of(owner_table.reshape(count))
    place = place_of(keys)
    stored = (place % replicas) * per_replica + place // replicas

    packed = pack(
        left_roots.reshape(slots, BS, BS), right_roots.reshape(slots, BS, BS)
    )
    roots = lax.all_to_all(
        packed.reshape(SIDE, capacity, 2, BS, BS),
        "shard",
        split_axis=0,
        concat_axis=0,
        axis_index_groups=MEMBERS,
        tiled=True,
    ).reshape(slots, 2, BS, BS)
    ordered = moved(place_kernel, stored, grads[0], [(count, BS, BS)], "place", (packed,))
    total = lax.psum_scatter(ordered, "rep", scatter_dimension=0, tiled=True)

    told = lax.ppermute(jnp.stack([keys, place]), everywhere, announce())
    sender_key, sender_place = told[0], told[1]
    serves = jnp.asarray(REPLICA_AT)[my_member, :, my_rep]
    slot_key = my_group * SIDE + jnp.arange(SIDE, dtype=jnp.int32)
    first = jnp.sum((sender_key[None, :] < slot_key[:, None]).astype(jnp.int32), axis=1)
    named = jnp.sum((sender_key[None, :] == slot_key[:, None]).astype(jnp.int32), axis=1)
    slot = jnp.arange(capacity, dtype=jnp.int32)
    slot_place = (first[:, None] + slot[None, :]).reshape(-1)
    slot_used = (slot[None, :] < named[:, None]).reshape(-1)
    taken = slot_used[None, :] & (slot_place[None, :] % replicas == serves[:, None])
    slot_order = jnp.arange(slots, dtype=jnp.int32)
    root_index = jnp.sum(jnp.where(taken, slot_order[None, :], 0), axis=1)

    held = serves[my_group] + replicas * jnp.arange(per_replica, dtype=jnp.int32)
    held_group = jnp.sum(
        jnp.where(sender_place[None, :] == held[:, None], sender_key[None, :], 0),
        axis=1,
    ) // SIDE

    roots = lax.all_to_all(
        pick(root_index, roots, "pick_roots"),
        "shard",
        split_axis=0,
        concat_axis=0,
        axis_index_groups=PEERS,
        tiled=True,
    )
    roots = pick(held_group, roots, "hold_roots")
    back = {b: a for a, b in aside()}
    roots = lax.ppermute(roots, everywhere, [(a, back[b]) for a, b in along_rep()])
    means, sizes = prepare(total, replicas)
    mine = precondition(means, sizes, roots)
    gathered = lax.all_gather(mine, "rep", axis=0, tiled=True)
    return moved(spread_kernel, stored, gathered, [(BS, width)], "spread")


def solution(mesh):
    placed = (
        P("rep", "shard", None),
        P("shard", None, None),
        P("shard", "rep", None, None, None),
        P("shard", "rep", None, None, None),
    )
    return jax.shard_map(
        local, mesh=mesh, in_specs=placed, out_specs=P("shard", None), check_vma=False
    )
```
